32 devices in a mesh: phase: 2 (over x), seq: 16 (over z, y, core).
Axes of the slice: x: 2, y: 2, z: 4, core: 2. Of those that a mesh axis runs over, the one named last changes fastest.
Arguments:
- tokens: bfloat16 [1024, 1024], P('seq'), may hold values from -6 to 6
- phase_weight: bfloat16 [2, 1024, 1024], P('phase'), may hold values from -0.1875 to 0.1875
- phase_gain: float32 [2, 1024], P('phase'), may hold values from 0.25 to 1.75
- unit_weight: bfloat16 [1024, 1024], replicated, may hold values from -0.1875 to 0.1875
- unit_gain: float32 [1024], replicated, may hold values from 0.25 to 1.75
- durations: int32 [1024], P('seq'), may hold values from 4 to 32, as said below
Outputs:
- encoder_out: bfloat16 [1024, 1024], P('seq')
- unit_states: bfloat16 [8192, 1024], P(('phase', 'seq'))
The draws below stay inside these ranges and needn't reach their ends.
Inputs may be any that keep to these rules, and one draw needn't show every extreme that they name: durations sum to 8192; some token has exactly 32 frames and some exactly 4.
All inputs are finite; a program needn't handle non-finite values.
Results may differ from the reference program's by a relative error of at most 0.0062.
Values may be sent and summed in bfloat16 or wider, within the bound.
A program may use at most 64 MiB of HBM per device.

```python
import jax
import jax.numpy as jnp
from jax import lax

D = 1024
TOKENS = 1024
FRAMES = 8192
DMIN = 4
DMAX = 32
LAYERS = 2


def draw_durations(key, part):
    key = jax.random.fold_in(key, 11)
    spare = DMAX - DMIN
    remain = FRAMES - TOKENS * DMIN
    key_pick, key_bias, key_score = jax.random.split(key, 3)
    picks = jax.random.permutation(key_pick, TOKENS)[:2]
    bias = jax.random.randint(key_bias, (TOKENS,), 0, 8)
    bias = bias.at[picks].set(-1)
    owner = jnp.repeat(jnp.arange(TOKENS, dtype=jnp.int32), spare)
    score = bias[owner] * 1024 + jax.random.randint(key_score, (TOKENS * spare,), 0, 1024)
    order = jnp.argsort(-score, stable=True)
    chosen = jnp.zeros((TOKENS * spare,), jnp.int32).at[order[:remain - spare]].set(1)
    extras = jax.ops.segment_sum(chosen, owner, num_segments=TOKENS)
    extras = extras.at[picks[0]].set(spare)
    return (DMIN + extras).astype(jnp.int32)


def level_of(own_key, dims, cuts, smallest, top_value):
    def one(position, shards_of):
        draws = jax.random.uniform(jax.random.fold_in(jax.random.fold_in(own_key, 6), position), (shards_of,), jnp.float32, smallest / len(cuts), top_value / len(cuts))
        return jnp.repeat(jnp.exp(draws), dims[position] // shards_of).reshape((-1,) + (1,) * (len(dims) - position - 1))

    factor_of = one(*cuts[0])
    for cut in cuts[1:]:
        factor_of = factor_of * one(*cut)
    return factor_of


def scatter_about(rng, extent, spread, reach, cuts=(), kind=jnp.bfloat16):
    loudness = level_of(rng, extent, cuts, -0.22, 0.18) if cuts else 1.0
    values = jax.random.normal(rng, extent, jnp.float32) * spread * loudness
    return jnp.minimum(jnp.maximum(values, -reach), reach).astype(kind)


def setup_inputs(seed: int = 0) -> dict:
    arg_keys = jax.random.split(jax.random.key(seed), 7)
    return {
        "tokens": scatter_about(arg_keys[0], (TOKENS, D), 1.0, 6.0, ((0, 16),)),
        "phase_weight": scatter_about(arg_keys[1], (LAYERS, D, D), D ** -0.5, 0.1875, ((0, 2),)),
        "phase_gain": jnp.clip(1.0 + 0.15 * jax.random.normal(arg_keys[2], (LAYERS, D), jnp.float32), 0.25, 1.75),
        "unit_weight": scatter_about(arg_keys[3], (D, D), D ** -0.5, 0.1875),
        "unit_gain": jnp.clip(1.0 + 0.15 * jax.random.normal(arg_keys[4], (D,), jnp.float32), 0.25, 1.75),
        "durations": draw_durations(jax.random.fold_in(arg_keys[6], 71), 0),
    }


def layer(values_in, weight, gain):
    widened = values_in.astype(jnp.float32)
    scaled = widened * gain / jnp.sqrt(lax.optimization_barrier(jnp.mean(widened * widened, axis=-1, keepdims=True)) + 1e-06)
    normed = scaled.astype(jnp.bfloat16)
    branch = jax.nn.silu(jnp.dot(normed, weight, preferred_element_type=jnp.float32))
    return (widened + branch).astype(jnp.bfloat16)

def reference(tokens, phase_weight, phase_gain, unit_weight, unit_gain, durations):
    hidden = tokens
    for layer_index in range(LAYERS):
        hidden = layer(hidden, phase_weight[layer_index], phase_gain[layer_index])
    expanded = jnp.repeat(hidden, durations, axis=0, total_repeat_length=FRAMES)
    return (hidden, layer(expanded, unit_weight, unit_gain))
```

```python
import functools

import jax
import jax.numpy as jnp
from jax import lax
from jax.experimental import pallas as pl
from jax.experimental.pallas import tpu as pltpu
from jax.sharding import PartitionSpec as P

FR_DEV = 256
COLS = 256
MESH = pl.DeviceIdType.MESH
BF = jnp.bfloat16
F32 = jnp.float32


def factors(seqsize):
    chips = seqsize // 2
    mid = 2 ** ((chips.bit_length() - 1) // 2)
    return chips // mid, mid


def kernel(
    phases, seqsize, slow, mid, rows,
    tokens, weight, gain, unit_weight, unit_gain, durations,
    enc_out, unit_out,
    w_buf, wu_buf, h_in, h_out, h_fin, held, member, total, o_buf, dur_all, durs_buf,
    load_sem, out_sem, relay_send, relay_recv, fin_send, fin_recv,
    dur_send, dur_recv2, dur_recv, up_send, down_send, mid_send, pair_send, recv_sem,
):
    width = tokens.shape[1]
    chunks = width // COLS
    plane = 2 * mid
    p = lax.axis_index("phase")
    s = lax.axis_index("seq")
    z = s // plane
    y = (s // 2) % mid
    c = s % 2
    last = p == phases - 1
    everyone = phases * seqsize
    frames = everyone * FR_DEV
    toks = rows * seqsize
    dmin = frames // (2 * toks)
    dmax = 8 * dmin

    def seq_of(zz, yy, cc):
        return zz * plane + yy * 2 + cc

    def bounds(zz):
        f0 = (p * seqsize + zz * plane) * FR_DEV
        f1 = f0 + plane * FR_DEV - 1
        low = jnp.maximum(f0 // dmax, toks - (frames - f0) // dmin)
        high = jnp.minimum(f1 // dmin, toks - ((frames - f1 - 1) // dmax + 1))
        low = jnp.minimum(low // rows, zz * plane)
        high = jnp.maximum(high // rows, zz * plane + plane - 1)
        return low, high

    low, high = bounds(z)
    low_up, _ = bounds(z + 1)
    _, high_down = bounds(z - 1)

    partners = [(p, seq_of(z, y, 1 - c))]
    partners += [(p, seq_of(z, (y + o) % mid, c)) for o in range(1, mid)]
    partners += [(p, seq_of((z + o) % slow, y, c)) for o in range(1, slow)]
    partners += [((p + o) % phases, s) for o in range(1, phases)]
    barrier = pltpu.get_barrier_semaphore()
    for target in partners:
        pl.semaphore_signal(barrier, inc=1, device_id=target, device_id_type=MESH)
    load_w = pltpu.make_async_copy(weight.at[0], w_buf, load_sem.at[0])
    load_w.start()
    load_wu = pltpu.make_async_copy(unit_weight, wu_buf, load_sem.at[1])
    load_wu.start()

    source = lax.broadcasted_iota(jnp.int32, (rows, 2 * rows), 0)
    lane = lax.broadcasted_iota(jnp.int32, (rows, 2 * rows), 1)
    place = (lane == source + c * rows).astype(BF)
    own = jnp.broadcast_to(durations[...], (8, rows)).astype(F32).astype(BF)
    own = jnp.dot(own, place, preferred_element_type=F32).astype(jnp.int32)
    dur_all[s] = own[0:1, :]

    for b in range(seqsize):
        @pl.when((b < low) | (b > high))
        def _():
            held[b * rows:(b + 1) * rows, :] = jnp.zeros((rows, width), BF)

    pl.semaphore_wait(barrier, len(partners))

    def dur_copy(start, size, sem, recv, target):
        return pltpu.make_async_remote_copy(
            src_ref=dur_all.at[pl.ds(start, size)], dst_ref=dur_all.at[pl.ds(start, size)],
            send_sem=sem, recv_sem=recv, device_id=target, device_id_type=MESH)

    dur_pair = dur_copy(s, 1, dur_send.at[0], dur_recv2.at[0], (p, seq_of(z, y, 1 - c)))
    dur_pair.start()

    def layer_chunks(source_ref, w_ref, gain_row, emit):
        v = source_ref[...].astype(F32)
        scale = lax.rsqrt(jnp.mean(v * v, axis=-1, keepdims=True) + 1e-06)
        normed = (v * gain_row * scale).astype(BF)
        for n in range(chunks):
            part = slice(n * COLS, (n + 1) * COLS)
            x = jnp.dot(normed, w_ref[:, part], preferred_element_type=F32)
            branch = 0.5 * x * (1.0 + jnp.tanh(0.5 * x))
            emit(n, part, (source_ref[:, part].astype(F32) + branch).astype(BF))

    def relay_copy(n):
        part = slice(n * COLS, (n + 1) * COLS)
        return pltpu.make_async_remote_copy(
            src_ref=h_out.at[:, part], dst_ref=h_in.at[:, part],
            send_sem=relay_send.at[n], recv_sem=relay_recv.at[n],
            device_id=((p + 1) % phases, s), device_id_type=MESH)

    def fin_copy(n, o):
        part = slice(n * COLS, (n + 1) * COLS)
        return pltpu.make_async_remote_copy(
            src_ref=h_fin.at[:, part], dst_ref=h_fin.at[:, part],
            send_sem=fin_send.at[n, o - 1], recv_sem=fin_recv.at[n],
            device_id=((p + o) % phases, s), device_id_type=MESH)

    def relay_emit(n, part, value):
        h_out[:, part] = value
        relay_copy(n).start()

    def fin_emit(n, part, value):
        h_fin[:, part] = value
        for o in range(1, phases):
            fin_copy(n, o).start()

    load_w.wait()

    @pl.when(p == 0)
    def _():
        layer_chunks(tokens, w_buf, gain[...], relay_emit if phases > 1 else fin_emit)

    dur_pair.wait()
    mids = [dur_copy(seq_of(z, y, 0), 2, dur_send.at[o], dur_recv2.at[o],
                     (p, seq_of(z, (y + o) % mid, c))) for o in range(1, mid)]
    for copy in mids:
        copy.start()
    for copy in mids:
        copy.wait()
    slows = [dur_copy(z * plane, plane, dur_send.at[mid - 1 + o], dur_recv.at[o],
                      (p, seq_of((z + o) % slow, y, c))) for o in range(1, slow)]
    for copy in slows:
        copy.start()
    for copy in slows:
        copy.wait()
    pairs = seqsize // 2
    for q in range(pairs):
        durs_buf[q:q + 1, :] = (dur_all[2 * q] + dur_all[2 * q + 1]).astype(F32)
    durs = durs_buf[...]
    tri = (lax.broadcasted_iota(jnp.int32, (2 * rows, 2 * rows), 0)
           <= lax.broadcasted_iota(jnp.int32, (2 * rows, 2 * rows), 1)).astype(BF)
    inner = jnp.dot(durs.astype(BF), tri, preferred_element_type=F32)
    frame = (lax.broadcasted_iota(jnp.int32, (FR_DEV, 2 * rows), 0)
             + (p * seqsize + s) * FR_DEV).astype(F32)
    before = jnp.zeros((1, 1), F32)
    for q in range(pairs):
        ends = inner[q:q + 1, :] + before
        begins = ends - durs[q:q + 1, :]
        inside = jnp.where((frame >= begins) & (frame < ends), 1.0, 0.0).astype(BF)
        at = (q % mid) * 2 * rows
        member[q // mid, :, at:at + 2 * rows] = inside
        before = before + jnp.sum(durs[q:q + 1, :], axis=1, keepdims=True)

    if phases > 1:
        @pl.when(p > 0)
        def _():
            for n in range(chunks):
                relay_copy(n).wait_recv()

            @pl.when(jnp.logical_not(last))
            def _():
                layer_chunks(h_in, w_buf, gain[...], relay_emit)

            @pl.when(last)
            def _():
                layer_chunks(h_in, w_buf, gain[...], fin_emit)

        @pl.when(jnp.logical_not(last))
        def _():
            for n in range(chunks):
                fin_copy(n, 1).wait_recv()

    enc_copy = pltpu.make_async_copy(h_fin, enc_out, out_sem.at[0])
    enc_copy.start()

    def block(b):
        return held.at[pl.ds(pl.multiple_of(b * rows, rows), rows)]

    def send(b, sem, target):
        return pltpu.make_async_remote_copy(
            src_ref=block(b), dst_ref=block(b), send_sem=sem, recv_sem=recv_sem.at[b],
            device_id=target, device_id_type=MESH)

    def up(zz):
        return send(seq_of(zz, y, c), up_send.at[zz], (p, seq_of((z + 1) % slow, y, c)))

    def down(zz):
        return send(seq_of(zz, y, c), down_send.at[zz], (p, seq_of((z + slow - 1) % slow, y, c)))

    def across(zz, o):
        return send(seq_of(zz, y, c), mid_send.at[zz, o], (p, seq_of(z, (y + o) % mid, c)))

    def sibling(b):
        return send(b, pair_send.at[b], (p, seq_of(z, y, 1 - c)))

    def goes_up(zz):
        return (z + 1 < slow) & (zz <= z) & (seq_of(zz, y, c) >= low_up)

    def goes_down(zz):
        return (z > 0) & (zz >= z) & (seq_of(zz, y, c) <= high_down)

    def wanted(b):
        return (b >= low) & (b <= high)

    load_wu.wait()

    def unit_emit(n, part, value):
        held[pl.ds(pl.multiple_of(s * rows, rows), rows), part] = value

    layer_chunks(h_fin, wu_buf, unit_gain[...], unit_emit)

    def spread_column(zz):
        @pl.when(goes_up(zz))
        def _():
            up(zz).start()

        @pl.when(goes_down(zz))
        def _():
            down(zz).start()

        for o in range(1, mid):
            across(zz, o).start()
        sibling(seq_of(zz, y, c)).start()

    def valid(zz):
        return (zz >= 0) & (zz < slow)

    def column(zz):
        @pl.when(valid(zz) & wanted(seq_of(zz, y, c)))
        def _():
            b = seq_of(zz, y, c)
            send(b, pair_send.at[b], (p, s)).wait_recv()
            spread_column(zz)

    def from_across(zz):
        for o in range(1, mid):
            b = seq_of(zz, (y + o) % mid, c)

            @pl.when(valid(zz) & wanted(b))
            def _():
                send(b, pair_send.at[b], (p, s)).wait_recv()
                sibling(b).start()

    def add_plane(zz, first):
        def work():
            for yy in range(mid):
                b = seq_of(zz, yy, 1 - c)

                @pl.when(wanted(b))
                def _():
                    send(b, pair_send.at[b], (p, s)).wait_recv()

            mask = member[zz]

            def one(n, carry):
                cols = pl.ds(pl.multiple_of(n * COLS, COLS), COLS)
                rows_at = pl.ds(pl.multiple_of(zz * plane * rows, plane * rows), plane * rows)
                got = jnp.dot(mask, held[rows_at, cols], preferred_element_type=F32)
                if first:
                    total[:, cols] = got
                else:
                    total[:, cols] += got
                return carry

            lax.fori_loop(0, chunks, one, 0)

        if first:
            work()
        else:
            pl.when(valid(zz) & (zz * plane + plane - 1 >= low) & (zz * plane <= high))(work)

    spread_column(z)
    for k in range(1, slow + 1):
        if k < slow:
            column(z - k)
            column(z + k)
        if k == 1:
            from_across(z)
            add_plane(z, True)
        else:
            for zz in (z - k + 1, z + k - 1):
                from_across(zz)
                add_plane(zz, False)

    out_copies = []
    part_rows = FR_DEV // 4
    for r in range(4):
        part = slice(r * part_rows, (r + 1) * part_rows)
        o_buf[part, :] = total[part, :].astype(BF)
        copy = pltpu.make_async_copy(o_buf.at[part], unit_out.at[part], out_sem.at[1 + r])
        copy.start()
        out_copies.append(copy)

    if phases > 1:
        @pl.when(jnp.logical_not(last))
        def _():
            for n in range(chunks):
                relay_copy(n).wait_send()

        @pl.when(last)
        def _():
            for n in range(chunks):
                for o in range(1, phases):
                    fin_copy(n, o).wait_send()

    for zz in range(slow):
        @pl.when(wanted(seq_of(zz, y, c)))
        def _():
            @pl.when(goes_up(zz))
            def _():
                up(zz).wait_send()

            @pl.when(goes_down(zz))
            def _():
                down(zz).wait_send()

            for o in range(1, mid):
                across(zz, o).wait_send()

        for yy in range(mid):
            b = seq_of(zz, yy, c)

            @pl.when(wanted(b))
            def _():
                sibling(b).wait_send()

    enc_copy.wait()
    for copy in out_copies:
        copy.wait()


def shards(tokens, phase_weight, phase_gain, unit_weight, unit_gain, durations):
    phases = lax.axis_size("phase")
    seqsize = lax.axis_size("seq")
    slow, mid = factors(seqsize)
    rows, width = tokens.shape
    chunks = width // COLS
    vmem = pl.BlockSpec(memory_space=pltpu.VMEM)
    anywhere = pl.BlockSpec(memory_space=pl.ANY)
    dma = pltpu.SemaphoreType.DMA
    return pl.pallas_call(
        functools.partial(kernel, phases, seqsize, slow, mid, rows),
        out_shape=(
            jax.ShapeDtypeStruct((rows, width), BF),
            jax.ShapeDtypeStruct((FR_DEV, width), BF),
        ),
        in_specs=[vmem, anywhere, vmem, anywhere, vmem, vmem],
        out_specs=(anywhere, anywhere),
        scratch_shapes=[
            pltpu.VMEM((width, width), BF),
            pltpu.VMEM((width, width), BF),
            pltpu.VMEM((rows, width), BF),
            pltpu.VMEM((rows, width), BF),
            pltpu.VMEM((rows, width), BF),
            pltpu.VMEM((rows * seqsize, width), BF),
            pltpu.VMEM((slow, FR_DEV, 2 * mid * rows), BF),
            pltpu.VMEM((FR_DEV, width), F32),
            pltpu.VMEM((FR_DEV, width), BF),
            pltpu.VMEM((seqsize, 1, 2 * rows), jnp.int32),
            pltpu.VMEM((seqsize // 2, 2 * rows), F32),
            dma((2,)),
            dma((5,)),
            dma((chunks,)),
            dma((chunks,)),
            dma((chunks, max(phases - 1, 1))),
            dma((chunks,)),
            dma((mid + slow,)),
            dma((mid,)),
            dma((slow,)),
            dma((slow,)),
            dma((slow,)),
            dma((slow, mid)),
            dma((seqsize,)),
            dma((seqsize,)),
        ],
        compiler_params=pltpu.CompilerParams(
            collective_id=0, has_side_effects=True, vmem_limit_bytes=40 * 1024 * 1024
        ),
        cost_estimate=pl.CostEstimate(
            flops=10 ** 9, bytes_accessed=8 * 10 ** 6, transcendentals=2 * 10 ** 5
        ),
    )(tokens, phase_weight, phase_gain, unit_weight, unit_gain.reshape(1, width),
      durations.reshape(1, rows))


def solution(mesh):
    return jax.shard_map(
        shards,
        mesh=mesh,
        in_specs=(P("seq", None), P("phase", None, None), P("phase", None), P(), P(), P("seq")),
        out_specs=(P("seq", None), P(("phase", "seq"), None)),
        check_vma=False,
    )
```

```python
import functools

import jax
import jax.numpy as jnp
from jax import lax
from jax.experimental import pallas as pl
from jax.experimental.pallas import tpu as pltpu
from jax.sharding import PartitionSpec as P

FR_DEV = 256
COLS = 256
MESH = pl.DeviceIdType.MESH
BF = jnp.bfloat16
F32 = jnp.float32


def factors(seqsize):
    chips = seqsize // 2
    mid = 2 ** ((chips.bit_length() - 1) // 2)
    return chips // mid, mid


def kernel(
    phases, seqsize, slow, mid, rows,
    tokens_hbm, weight, gain_hbm, unit_weight, unit_gain_hbm, durations_hbm,
    enc_out, unit_out,
    tokens, gain, unit_gain, durations, w_buf, wu_buf, h_in, h_out, h_fin, held, member, total, o_buf, dur_all, durs_buf,
    load_sem, out_sem, relay_send, relay_recv, fin_send, fin_recv,
    dur_send, dur_near, dur_recv, up_send, down_send, mid_send, pair_send, recv_sem,
):
    width = tokens.shape[1]
    chunks = width // COLS
    plane = 2 * mid
    p = lax.axis_index("phase")
    s = lax.axis_index("seq")
    z = s // plane
    y = (s // 2) % mid
    c = s % 2
    last = p == phases - 1
    everyone = phases * seqsize
    frames = everyone * FR_DEV
    toks = rows * seqsize
    dmin = frames // (2 * toks)
    dmax = 8 * dmin

    def seq_of(zz, yy, cc):
        return zz * plane + yy * 2 + cc

    def bounds(zz):
        f0 = (p * seqsize + zz * plane) * FR_DEV
        f1 = f0 + plane * FR_DEV - 1
        low = jnp.maximum(f0 // dmax, toks - (frames - f0) // dmin)
        high = jnp.minimum(f1 // dmin, toks - ((frames - f1 - 1) // dmax + 1))
        low = jnp.minimum(low // rows, zz * plane)
        high = jnp.maximum(high // rows, zz * plane + plane - 1)
        return low, high

    low, high = bounds(z)
    low_up, _ = bounds(z + 1)
    _, high_down = bounds(z - 1)

    partners = [(p, seq_of(z, y, 1 - c))]
    partners += [(p, seq_of(z, (y + o) % mid, cc)) for o in range(1, mid) for cc in (c, 1 - c)]
    partners += [(p, seq_of((z + o) % slow, y, c)) for o in range(1, slow)]
    partners += [((p + o) % phases, s) for o in range(1, phases)]
    barrier = pltpu.get_barrier_semaphore()
    for target in partners:
        pl.semaphore_signal(barrier, inc=1, device_id=target, device_id_type=MESH)
    loads = [
        pltpu.make_async_copy(source, target, load_sem.at[2 + i])
        for i, (source, target) in enumerate([
            (durations_hbm, durations), (tokens_hbm, tokens), (gain_hbm, gain),
            (unit_gain_hbm, unit_gain)])
    ]
    for load in loads:
        load.start()
    load_w = pltpu.make_async_copy(weight.at[0], w_buf, load_sem.at[0])
    load_w.start()
    load_wu = pltpu.make_async_copy(unit_weight, wu_buf, load_sem.at[1])
    load_wu.start()

    loads[0].wait()
    source = lax.broadcasted_iota(jnp.int32, (rows, 2 * rows), 0)
    lane = lax.broadcasted_iota(jnp.int32, (rows, 2 * rows), 1)
    place = (lane == source + c * rows).astype(BF)
    own = jnp.broadcast_to(durations[...], (8, rows)).astype(F32).astype(BF)
    own = jnp.dot(own, place, preferred_element_type=F32).astype(jnp.int32)
    dur_all[s] = own[0:1, :]

    for b in range(seqsize):
        @pl.when((b < low) | (b > high))
        def _():
            held[b * rows:(b + 1) * rows, :] = jnp.zeros((rows, width), BF)

    pl.semaphore_wait(barrier, len(partners))

    def dur_copy(start, size, sem, recv, target):
        return pltpu.make_async_remote_copy(
            src_ref=dur_all.at[pl.ds(start, size)], dst_ref=dur_all.at[pl.ds(start, size)],
            send_sem=sem, recv_sem=recv, device_id=target, device_id_type=MESH)

    def near(i):
        return dur_copy(s, 1, dur_send.at[i], dur_near.at[i], (p, seq_of(
            z, (y + (i + 1) // 2) % mid, (c + i + 1) % 2)))

    for i in range(plane - 1):
        near(i).start()

    def layer_chunks(source_ref, w_ref, gain_row, emit):
        v = source_ref[...].astype(F32)
        scale = lax.rsqrt(jnp.mean(v * v, axis=-1, keepdims=True) + 1e-06)
        normed = (v * gain_row * scale).astype(BF)
        for n in range(chunks):
            part = slice(n * COLS, (n + 1) * COLS)
            x = jnp.dot(normed, w_ref[:, part], preferred_element_type=F32)
            branch = 0.5 * x * (1.0 + jnp.tanh(0.5 * x))
            emit(n, part, (source_ref[:, part].astype(F32) + branch).astype(BF))

    def relay_copy(n):
        part = slice(n * COLS, (n + 1) * COLS)
        return pltpu.make_async_remote_copy(
            src_ref=h_out.at[:, part], dst_ref=h_in.at[:, part],
            send_sem=relay_send.at[n], recv_sem=relay_recv.at[n],
            device_id=((p + 1) % phases, s), device_id_type=MESH)

    def fin_copy(n, o):
        part = slice(n * COLS, (n + 1) * COLS)
        return pltpu.make_async_remote_copy(
            src_ref=h_fin.at[:, part], dst_ref=h_fin.at[:, part],
            send_sem=fin_send.at[n, o - 1], recv_sem=fin_recv.at[n],
            device_id=((p + o) % phases, s), device_id_type=MESH)

    def relay_emit(n, part, value):
        h_out[:, part] = value
        relay_copy(n).start()

    def fin_emit(n, part, value):
        h_fin[:, part] = value
        for o in range(1, phases):
            fin_copy(n, o).start()

    for load in loads[1:]:
        load.wait()
    load_w.wait()

    @pl.when(p == 0)
    def _():
        layer_chunks(tokens, w_buf, gain[...], relay_emit if phases > 1 else fin_emit)

    def far(o):
        return dur_copy(z * plane, plane, dur_send.at[plane - 1 + o], dur_recv.at[o],
                        (p, seq_of((z + o) % slow, y, c)))

    for i in range(plane - 1):
        near(i).wait()
    for o in range(1, slow):
        far(o).start()

    def make_member():
        for o in range(1, slow):
            far(o).wait()
        pairs = seqsize // 2
        for q in range(pairs):
            durs_buf[q:q + 1, :] = (dur_all[2 * q] + dur_all[2 * q + 1]).astype(F32)
        durs = durs_buf[...]
        tri = (lax.broadcasted_iota(jnp.int32, (2 * rows, 2 * rows), 0)
               <= lax.broadcasted_iota(jnp.int32, (2 * rows, 2 * rows), 1)).astype(BF)
        inner = jnp.dot(durs.astype(BF), tri, preferred_element_type=F32)
        frame = (lax.broadcasted_iota(jnp.int32, (FR_DEV, 2 * rows), 0)
                 + (p * seqsize + s) * FR_DEV).astype(F32)
        before = jnp.zeros((1, 1), F32)
        for q in range(pairs):
            ends = inner[q:q + 1, :] + before
            begins = ends - durs[q:q + 1, :]
            inside = jnp.where((frame >= begins) & (frame < ends), 1.0, 0.0).astype(BF)
            at = (q % mid) * 2 * rows
            member[q // mid, :, at:at + 2 * rows] = inside
            before = before + jnp.sum(durs[q:q + 1, :], axis=1, keepdims=True)

    pl.when(jnp.logical_not(last))(make_member)

    if phases > 1:
        @pl.when(p > 0)
        def _():
            for n in range(chunks):
                relay_copy(n).wait_recv()

            @pl.when(jnp.logical_not(last))
            def _():
                layer_chunks(h_in, w_buf, gain[...], relay_emit)

            @pl.when(last)
            def _():
                layer_chunks(h_in, w_buf, gain[...], fin_emit)

        @pl.when(jnp.logical_not(last))
        def _():
            for n in range(chunks):
                fin_copy(n, 1).wait_recv()

    enc_copy = pltpu.make_async_copy(h_fin, enc_out, out_sem.at[0])
    enc_copy.start()

    def block(b):
        return held.at[pl.ds(pl.multiple_of(b * rows, rows), rows)]

    def send(b, sem, target):
        return pltpu.make_async_remote_copy(
            src_ref=block(b), dst_ref=block(b), send_sem=sem, recv_sem=recv_sem.at[b],
            device_id=target, device_id_type=MESH)

    def up(zz):
        return send(seq_of(zz, y, c), up_send.at[zz], (p, seq_of((z + 1) % slow, y, c)))

    def down(zz):
        return send(seq_of(zz, y, c), down_send.at[zz], (p, seq_of((z + slow - 1) % slow, y, c)))

    def across(zz, o):
        return send(seq_of(zz, y, c), mid_send.at[zz, o], (p, seq_of(z, (y + o) % mid, c)))

    def sibling(b):
        return send(b, pair_send.at[b], (p, seq_of(z, y, 1 - c)))

    def goes_up(zz):
        return (z + 1 < slow) & (zz <= z) & (seq_of(zz, y, c) >= low_up)

    def goes_down(zz):
        return (z > 0) & (zz >= z) & (seq_of(zz, y, c) <= high_down)

    def wanted(b):
        return (b >= low) & (b <= high)

    load_wu.wait()

    def unit_emit(n, part, value):
        held[pl.ds(pl.multiple_of(s * rows, rows), rows), part] = value

    layer_chunks(h_fin, wu_buf, unit_gain[...], unit_emit)

    def spread_column(zz):
        @pl.when(goes_up(zz))
        def _():
            up(zz).start()

        @pl.when(goes_down(zz))
        def _():
            down(zz).start()

        for o in range(1, mid):
            across(zz, o).start()
        sibling(seq_of(zz, y, c)).start()

    def valid(zz):
        return (zz >= 0) & (zz < slow)

    def column(zz):
        @pl.when(valid(zz) & wanted(seq_of(zz, y, c)))
        def _():
            b = seq_of(zz, y, c)
            send(b, pair_send.at[b], (p, s)).wait_recv()
            spread_column(zz)

    def from_across(zz):
        for o in range(1, mid):
            b = seq_of(zz, (y + o) % mid, c)

            @pl.when(valid(zz) & wanted(b))
            def _():
                send(b, pair_send.at[b], (p, s)).wait_recv()
                sibling(b).start()

    def add_plane(zz, first):
        def work():
            for yy in range(mid):
                b = seq_of(zz, yy, 1 - c)

                @pl.when(wanted(b))
                def _():
                    send(b, pair_send.at[b], (p, s)).wait_recv()

            mask = member[zz]

            def one(n, carry):
                cols = pl.ds(pl.multiple_of(n * COLS, COLS), COLS)
                rows_at = pl.ds(pl.multiple_of(zz * plane * rows, plane * rows), plane * rows)
                got = jnp.dot(mask, held[rows_at, cols], preferred_element_type=F32)
                if first:
                    total[:, cols] = got
                else:
                    total[:, cols] += got
                return carry

            lax.fori_loop(0, chunks, one, 0)

        if first:
            work()
        else:
            pl.when(valid(zz) & (zz * plane + plane - 1 >= low) & (zz * plane <= high))(work)

    spread_column(z)
    pl.when(last)(make_member)
    for k in range(1, slow + 1):
        if k < slow:
            column(z - k)
            column(z + k)
        if k == 1:
            from_across(z)
            add_plane(z, True)
        else:
            for zz in (z - k + 1, z + k - 1):
                from_across(zz)
                add_plane(zz, False)

    out_copies = []
    part_rows = FR_DEV // 4
    for r in range(4):
        part = slice(r * part_rows, (r + 1) * part_rows)
        o_buf[part, :] = total[part, :].astype(BF)
        copy = pltpu.make_async_copy(o_buf.at[part], unit_out.at[part], out_sem.at[1 + r])
        copy.start()
        out_copies.append(copy)

    if phases > 1:
        @pl.when(jnp.logical_not(last))
        def _():
            for n in range(chunks):
                relay_copy(n).wait_send()

        @pl.when(last)
        def _():
            for n in range(chunks):
                for o in range(1, phases):
                    fin_copy(n, o).wait_send()

    for zz in range(slow):
        @pl.when(wanted(seq_of(zz, y, c)))
        def _():
            @pl.when(goes_up(zz))
            def _():
                up(zz).wait_send()

            @pl.when(goes_down(zz))
            def _():
                down(zz).wait_send()

            for o in range(1, mid):
                across(zz, o).wait_send()

        for yy in range(mid):
            b = seq_of(zz, yy, c)

            @pl.when(wanted(b))
            def _():
                sibling(b).wait_send()

    enc_copy.wait()
    for copy in out_copies:
        copy.wait()


def shards(tokens, phase_weight, phase_gain, unit_weight, unit_gain, durations):
    phases = lax.axis_size("phase")
    seqsize = lax.axis_size("seq")
    slow, mid = factors(seqsize)
    rows, width = tokens.shape
    chunks = width // COLS
    anywhere = pl.BlockSpec(memory_space=pl.ANY)
    hbm = pl.BlockSpec(memory_space=pltpu.HBM)
    dma = pltpu.SemaphoreType.DMA
    return pl.pallas_call(
        functools.partial(kernel, phases, seqsize, slow, mid, rows),
        out_shape=(
            jax.ShapeDtypeStruct((rows, width), BF),
            jax.ShapeDtypeStruct((FR_DEV, width), BF),
        ),
        in_specs=[hbm] * 6,
        out_specs=(anywhere, anywhere),
        scratch_shapes=[
            pltpu.VMEM((rows, width), BF),
            pltpu.VMEM((1, width), F32),
            pltpu.VMEM((1, width), F32),
            pltpu.VMEM((1, rows), jnp.int32),
            pltpu.VMEM((width, width), BF),
            pltpu.VMEM((width, width), BF),
            pltpu.VMEM((rows, width), BF),
            pltpu.VMEM((rows, width), BF),
            pltpu.VMEM((rows, width), BF),
            pltpu.VMEM((rows * seqsize, width), BF),
            pltpu.VMEM((slow, FR_DEV, 2 * mid * rows), BF),
            pltpu.VMEM((FR_DEV, width), F32),
            pltpu.VMEM((FR_DEV, width), BF),
            pltpu.VMEM((seqsize, 1, 2 * rows), jnp.int32),
            pltpu.VMEM((seqsize // 2, 2 * rows), F32),
            dma((6,)),
            dma((5,)),
            dma((chunks,)),
            dma((chunks,)),
            dma((chunks, max(phases - 1, 1))),
            dma((chunks,)),
            dma((2 * mid + slow,)),
            dma((2 * mid,)),
            dma((slow,)),
            dma((slow,)),
            dma((slow,)),
            dma((slow, mid)),
            dma((seqsize,)),
            dma((seqsize,)),
        ],
        compiler_params=pltpu.CompilerParams(
            collective_id=0, has_side_effects=True, vmem_limit_bytes=63 * 1024 * 1024
        ),
        cost_estimate=pl.CostEstimate(
            flops=10 ** 9, bytes_accessed=8 * 10 ** 6, transcendentals=2 * 10 ** 5
        ),
    )(tokens, phase_weight, phase_gain, unit_weight, unit_gain.reshape(1, width),
      durations.reshape(1, rows))


def solution(mesh):
    return jax.shard_map(
        shards,
        mesh=mesh,
        in_specs=(P("seq", None), P("phase", None, None), P("phase", None), P(), P(), P("seq")),
        out_specs=(P("seq", None), P(("phase", "seq"), None)),
        check_vma=False,
    )
```

```python
import functools

import jax
import jax.numpy as jnp
from jax import lax
from jax.experimental import pallas as pl
from jax.experimental.pallas import tpu as pltpu
from jax.sharding import PartitionSpec as P

FR_DEV = 256
COLS = 256
HALVES = 2
MESH = pl.DeviceIdType.MESH
BF = jnp.bfloat16
F32 = jnp.float32


def factors(seqsize):
    chips = seqsize // 2
    mid = 2 ** ((chips.bit_length() - 1) // 2)
    return chips // mid, mid


def kernel(
    phases, seqsize, slow, mid, rows,
    tokens_hbm, weight, gain_hbm, unit_weight, unit_gain_hbm, durations_hbm,
    enc_out, unit_out,
    tokens, gain, unit_gain, durations, w_buf, wu_buf, h_in, h_out, h_fin, held, member, total, o_buf, dur_all, durs_buf,
    load_sem, out_sem, relay_send, relay_recv, fin_send, fin_recv,
    dur_send, dur_near, dur_recv, up_send, down_send, mid_send, pair_send, recv_sem,
):
    width = tokens.shape[1]
    chunks = width // COLS
    plane = 2 * mid
    p = lax.axis_index("phase")
    s = lax.axis_index("seq")
    z = s // plane
    y = (s // 2) % mid
    c = s % 2
    last = p == phases - 1
    everyone = phases * seqsize
    frames = everyone * FR_DEV
    toks = rows * seqsize
    dmin = frames // (2 * toks)
    dmax = 8 * dmin

    def seq_of(zz, yy, cc):
        return zz * plane + yy * 2 + cc

    def bounds(zz):
        f0 = (p * seqsize + zz * plane) * FR_DEV
        f1 = f0 + plane * FR_DEV - 1
        low = jnp.maximum(f0 // dmax, toks - (frames - f0) // dmin)
        high = jnp.minimum(f1 // dmin, toks - ((frames - f1 - 1) // dmax + 1))
        low = jnp.minimum(low // rows, zz * plane)
        high = jnp.maximum(high // rows, zz * plane + plane - 1)
        return low, high

    low, high = bounds(z)
    low_up, _ = bounds(z + 1)
    _, high_down = bounds(z - 1)

    partners = [(p, seq_of(z, y, 1 - c))]
    partners += [(p, seq_of(z, (y + o) % mid, cc)) for o in range(1, mid) for cc in (c, 1 - c)]
    partners += [(p, seq_of((z + o) % slow, y, c)) for o in range(1, slow)]
    partners += [((p + o) % phases, s) for o in range(1, phases)]
    barrier = pltpu.get_barrier_semaphore()
    for target in partners:
        pl.semaphore_signal(barrier, inc=1, device_id=target, device_id_type=MESH)
    loads = [
        pltpu.make_async_copy(source, target, load_sem.at[2 + i])
        for i, (source, target) in enumerate([
            (durations_hbm, durations), (tokens_hbm, tokens), (gain_hbm, gain),
            (unit_gain_hbm, unit_gain)])
    ]
    for load in loads:
        load.start()
    load_w = pltpu.make_async_copy(weight.at[0], w_buf, load_sem.at[0])
    load_w.start()
    load_wu = pltpu.make_async_copy(unit_weight, wu_buf, load_sem.at[1])

    loads[0].wait()
    source = lax.broadcasted_iota(jnp.int32, (rows, 2 * rows), 0)
    lane = lax.broadcasted_iota(jnp.int32, (rows, 2 * rows), 1)
    place = (lane == source + c * rows).astype(BF)
    own = jnp.broadcast_to(durations[...], (8, rows)).astype(F32).astype(BF)
    own = jnp.dot(own, place, preferred_element_type=F32).astype(jnp.int32)
    dur_all[s] = own[0:1, :]

    for b in range(seqsize):
        @pl.when((b < low) | (b > high))
        def _():
            held[b * rows:(b + 1) * rows, :] = jnp.zeros((rows, width), BF)

    pl.semaphore_wait(barrier, len(partners))

    def dur_copy(start, size, sem, recv, target):
        return pltpu.make_async_remote_copy(
            src_ref=dur_all.at[pl.ds(start, size)], dst_ref=dur_all.at[pl.ds(start, size)],
            send_sem=sem, recv_sem=recv, device_id=target, device_id_type=MESH)

    def near(i):
        return dur_copy(s, 1, dur_send.at[i], dur_near.at[i], (p, seq_of(
            z, (y + (i + 1) // 2) % mid, (c + i + 1) % 2)))

    for i in range(plane - 1):
        near(i).start()

    def layer_chunks(source_ref, w_ref, gain_row, emit):
        v = source_ref[...].astype(F32)
        scale = lax.rsqrt(jnp.mean(v * v, axis=-1, keepdims=True) + 1e-06)
        normed = (v * gain_row * scale).astype(BF)
        for n in range(chunks):
            part = slice(n * COLS, (n + 1) * COLS)
            x = jnp.dot(normed, w_ref[:, part], preferred_element_type=F32)
            branch = 0.5 * x * (1.0 + jnp.tanh(0.5 * x))
            emit(n, part, (source_ref[:, part].astype(F32) + branch).astype(BF))

    def relay_copy(n):
        part = slice(n * COLS, (n + 1) * COLS)
        return pltpu.make_async_remote_copy(
            src_ref=h_out.at[:, part], dst_ref=h_in.at[:, part],
            send_sem=relay_send.at[n], recv_sem=relay_recv.at[n],
            device_id=((p + 1) % phases, s), device_id_type=MESH)

    def fin_copy(n, o):
        part = slice(n * COLS, (n + 1) * COLS)
        return pltpu.make_async_remote_copy(
            src_ref=h_fin.at[:, part], dst_ref=h_fin.at[:, part],
            send_sem=fin_send.at[n, o - 1], recv_sem=fin_recv.at[n],
            device_id=((p + o) % phases, s), device_id_type=MESH)

    def relay_emit(n, part, value):
        h_out[:, part] = value
        relay_copy(n).start()

    def fin_emit(n, part, value):
        h_fin[:, part] = value
        for o in range(1, phases):
            fin_copy(n, o).start()

    for load in loads[1:]:
        load.wait()
    load_w.wait()
    load_wu.start()

    @pl.when(p == 0)
    def _():
        layer_chunks(tokens, w_buf, gain[...], relay_emit if phases > 1 else fin_emit)

    def far(o):
        return dur_copy(z * plane, plane, dur_send.at[plane - 1 + o], dur_recv.at[o],
                        (p, seq_of((z + o) % slow, y, c)))

    for i in range(plane - 1):
        near(i).wait()
    for o in range(1, slow):
        far(o).start()

    def make_member():
        for o in range(1, slow):
            far(o).wait()
        pairs = seqsize // 2
        for q in range(pairs):
            durs_buf[q:q + 1, :] = (dur_all[2 * q] + dur_all[2 * q + 1]).astype(F32)
        durs = durs_buf[...]
        tri = (lax.broadcasted_iota(jnp.int32, (2 * rows, 2 * rows), 0)
               <= lax.broadcasted_iota(jnp.int32, (2 * rows, 2 * rows), 1)).astype(BF)
        inner = jnp.dot(durs.astype(BF), tri, preferred_element_type=F32)
        frame = (lax.broadcasted_iota(jnp.int32, (FR_DEV, 2 * rows), 0)
                 + (p * seqsize + s) * FR_DEV).astype(F32)
        before = jnp.zeros((1, 1), F32)
        for q in range(pairs):
            ends = inner[q:q + 1, :] + before
            begins = ends - durs[q:q + 1, :]
            inside = jnp.where((frame >= begins) & (frame < ends), 1.0, 0.0).astype(BF)
            at = (q % mid) * 2 * rows
            member[q // mid, :, at:at + 2 * rows] = inside
            before = before + jnp.sum(durs[q:q + 1, :], axis=1, keepdims=True)

    pl.when(jnp.logical_not(last))(make_member)

    if phases > 1:
        @pl.when(p > 0)
        def _():
            for n in range(chunks):
                relay_copy(n).wait_recv()

            @pl.when(jnp.logical_not(last))
            def _():
                layer_chunks(h_in, w_buf, gain[...], relay_emit)

            @pl.when(last)
            def _():
                layer_chunks(h_in, w_buf, gain[...], fin_emit)

        @pl.when(jnp.logical_not(last))
        def _():
            for n in range(chunks):
                fin_copy(n, 1).wait_recv()

    enc_copy = pltpu.make_async_copy(h_fin, enc_out, out_sem.at[0])
    enc_copy.start()

    half = width // HALVES

    def block(b, h):
        return held.at[pl.ds(pl.multiple_of(b * rows, rows), rows), h * half:(h + 1) * half]

    def send(b, h, sem, target):
        return pltpu.make_async_remote_copy(
            src_ref=block(b, h), dst_ref=block(b, h), send_sem=sem, recv_sem=recv_sem.at[b, h],
            device_id=target, device_id_type=MESH)

    def up(zz, h):
        return send(seq_of(zz, y, c), h, up_send.at[zz, h], (p, seq_of((z + 1) % slow, y, c)))

    def down(zz, h):
        return send(seq_of(zz, y, c), h, down_send.at[zz, h],
                    (p, seq_of((z + slow - 1) % slow, y, c)))

    def across(zz, o, h):
        return send(seq_of(zz, y, c), h, mid_send.at[zz, o, h], (p, seq_of(z, (y + o) % mid, c)))

    def sibling(b, h):
        return send(b, h, pair_send.at[b, h], (p, seq_of(z, y, 1 - c)))

    def arrived(b, h):
        sibling(b, h).wait_recv()

    def goes_up(zz):
        return (z + 1 < slow) & (zz <= z) & (seq_of(zz, y, c) >= low_up)

    def goes_down(zz):
        return (z > 0) & (zz >= z) & (seq_of(zz, y, c) <= high_down)

    def wanted(b):
        return (b >= low) & (b <= high)

    def valid(zz):
        return (zz >= 0) & (zz < slow)

    def spread_column(zz, h):
        @pl.when(goes_up(zz))
        def _():
            up(zz, h).start()

        @pl.when(goes_down(zz))
        def _():
            down(zz, h).start()

        for o in range(1, mid):
            across(zz, o, h).start()
        sibling(seq_of(zz, y, c), h).start()

    load_wu.wait()

    def unit_emit(n, part, value):
        held[pl.ds(pl.multiple_of(s * rows, rows), rows), part] = value
        if (n + 1) * COLS % half == 0:
            spread_column(z, n * COLS // half)

    layer_chunks(h_fin, wu_buf, unit_gain[...], unit_emit)

    def column(zz, h):
        b = seq_of(zz, y, c)

        @pl.when(valid(zz) & wanted(b))
        def _():
            arrived(b, h)
            spread_column(zz, h)

    def from_across(zz, h):
        for o in range(1, mid):
            b = seq_of(zz, (y + o) % mid, c)

            @pl.when(valid(zz) & wanted(b))
            def _():
                arrived(b, h)
                sibling(b, h).start()

    def add_plane(zz, h, first):
        def work():
            for yy in range(mid):
                b = seq_of(zz, yy, 1 - c)

                @pl.when(wanted(b))
                def _():
                    arrived(b, h)

            mask = member[zz]
            rows_at = pl.ds(pl.multiple_of(zz * plane * rows, plane * rows), plane * rows)
            for n in range(h * half // COLS, (h + 1) * half // COLS):
                cols = slice(n * COLS, (n + 1) * COLS)
                got = jnp.dot(mask, held[rows_at, cols], preferred_element_type=F32)
                if first:
                    total[:, cols] = got
                else:
                    total[:, cols] += got

        if first:
            work()
        else:
            pl.when(valid(zz) & (zz * plane + plane - 1 >= low) & (zz * plane <= high))(work)

    pl.when(last)(make_member)
    out_copies = []
    steps = [(k, h) for k in range(slow) for h in range(HALVES)]
    for i in range(HALVES, len(steps) + 4):
        if i < len(steps):
            k, h = steps[i]
            column(z - k, h)
            column(z + k, h)
        if i == HALVES:
            for h in range(HALVES - 1):
                from_across(z, h)
        if i - 1 < len(steps):
            k, h = steps[i - 1]
            for zz in (z - k, z + k) if k else (z,):
                from_across(zz, h)
        if 0 <= i - 4 < len(steps):
            k, h = steps[i - 4]
            for zz in (z - k, z + k) if k else (z,):
                add_plane(zz, h, k == 0)
            if k == slow - 1:
                part = slice(h * half, (h + 1) * half)
                o_buf[:, part] = total[:, part].astype(BF)
                copy = pltpu.make_async_copy(o_buf.at[:, part], unit_out.at[:, part],
                                             out_sem.at[1 + h])
                copy.start()
                out_copies.append(copy)

    if phases > 1:
        @pl.when(jnp.logical_not(last))
        def _():
            for n in range(chunks):
                relay_copy(n).wait_send()

        @pl.when(last)
        def _():
            for n in range(chunks):
                for o in range(1, phases):
                    fin_copy(n, o).wait_send()

    for zz in range(slow):
        @pl.when(wanted(seq_of(zz, y, c)))
        def _():
            for h in range(HALVES):
                @pl.when(goes_up(zz))
                def _():
                    up(zz, h).wait_send()

                @pl.when(goes_down(zz))
                def _():
                    down(zz, h).wait_send()

                for o in range(1, mid):
                    across(zz, o, h).wait_send()

        for yy in range(mid):
            b = seq_of(zz, yy, c)

            @pl.when(wanted(b))
            def _():
                for h in range(HALVES):
                    sibling(b, h).wait_send()

    enc_copy.wait()
    for copy in out_copies:
        copy.wait()


def shards(tokens, phase_weight, phase_gain, unit_weight, unit_gain, durations):
    phases = lax.axis_size("phase")
    seqsize = lax.axis_size("seq")
    slow, mid = factors(seqsize)
    rows, width = tokens.shape
    chunks = width // COLS
    anywhere = pl.BlockSpec(memory_space=pl.ANY)
    hbm = pl.BlockSpec(memory_space=pltpu.HBM)
    dma = pltpu.SemaphoreType.DMA
    return pl.pallas_call(
        functools.partial(kernel, phases, seqsize, slow, mid, rows),
        out_shape=(
            pltpu.VMEM((rows, width), BF),
            pltpu.VMEM((FR_DEV, width), BF),
        ),
        in_specs=[hbm] * 6,
        out_specs=(anywhere, anywhere),
        scratch_shapes=[
            pltpu.VMEM((rows, width), BF),
            pltpu.VMEM((1, width), F32),
            pltpu.VMEM((1, width), F32),
            pltpu.VMEM((1, rows), jnp.int32),
            pltpu.VMEM((width, width), BF),
            pltpu.VMEM((width, width), BF),
            pltpu.VMEM((rows, width), BF),
            pltpu.VMEM((rows, width), BF),
            pltpu.VMEM((rows, width), BF),
            pltpu.VMEM((rows * seqsize, width), BF),
            pltpu.VMEM((slow, FR_DEV, 2 * mid * rows), BF),
            pltpu.VMEM((FR_DEV, width), F32),
            pltpu.VMEM((FR_DEV, width), BF),
            pltpu.VMEM((seqsize, 1, 2 * rows), jnp.int32),
            pltpu.VMEM((seqsize // 2, 2 * rows), F32),
            dma((6,)),
            dma((5,)),
            dma((chunks,)),
            dma((chunks,)),
            dma((chunks, max(phases - 1, 1))),
            dma((chunks,)),
            dma((2 * mid + slow,)),
            dma((2 * mid,)),
            dma((slow,)),
            dma((slow, HALVES)),
            dma((slow, HALVES)),
            dma((slow, mid, HALVES)),
            dma((seqsize, HALVES)),
            dma((seqsize, HALVES)),
        ],
        compiler_params=pltpu.CompilerParams(
            collective_id=0, has_side_effects=True, vmem_limit_bytes=40 * 1024 * 1024
        ),
        cost_estimate=pl.CostEstimate(
            flops=10 ** 9, bytes_accessed=8 * 10 ** 6, transcendentals=2 * 10 ** 5
        ),
    )(*[pltpu.with_memory_space_constraint(a, pltpu.HBM) for a in (tokens, phase_weight, phase_gain, unit_weight, unit_gain.reshape(1, width),
      durations.reshape(1, rows))])


def solution(mesh):
    return jax.shard_map(
        shards,
        mesh=mesh,
        in_specs=(P("seq", None), P("phase", None, None), P("phase", None), P(), P(), P("seq")),
        out_specs=(P("seq", None), P(("phase", "seq"), None)),
        check_vma=False,
    )
```

```python
import functools

import jax
import jax.numpy as jnp
from jax import lax
from jax.experimental import pallas as pl
from jax.experimental.pallas import tpu as pltpu
from jax.sharding import PartitionSpec as P

FR_DEV = 256
COLS = 256
HALVES = 2
MESH = pl.DeviceIdType.MESH
BF = jnp.bfloat16
F32 = jnp.float32


def factors(seqsize):
    chips = seqsize // 2
    mid = 2 ** ((chips.bit_length() - 1) // 2)
    return chips // mid, mid


def kernel(
    phases, seqsize, slow, mid, rows,
    tokens_hbm, weight, gain_hbm, unit_weight, unit_gain_hbm, durations_hbm,
    enc_out, unit_out,
    tokens, gain, unit_gain, durations, w_buf, wu_buf, h_in, h_out, h_fin, held, member, total, o_buf, dur_all, durs_buf,
    load_sem, out_sem, relay_send, relay_recv, fin_send, fin_recv,
    dur_send, dur_near, dur_recv, up_send, down_send, mid_send, pair_send, recv_sem,
):
    width = tokens.shape[1]
    chunks = width // COLS
    plane = 2 * mid
    p = lax.axis_index("phase")
    s = lax.axis_index("seq")
    z = s // plane
    y = (s // 2) % mid
    c = s % 2
    last = p == phases - 1
    everyone = phases * seqsize
    frames = everyone * FR_DEV
    toks = rows * seqsize
    dmin = frames // (2 * toks)
    dmax = 8 * dmin

    def seq_of(zz, yy, cc):
        return zz * plane + yy * 2 + cc

    def needed(first, count):
        f0 = (p * seqsize + first) * FR_DEV
        f1 = f0 + count * FR_DEV - 1
        low = jnp.maximum(f0 // dmax, toks - (frames - f0) // dmin)
        high = jnp.minimum(f1 // dmin, toks - ((frames - f1 - 1) // dmax + 1))
        return low // rows, high // rows

    def bounds(zz):
        low, high = needed(zz * plane, plane)
        return jnp.minimum(low, zz * plane), jnp.maximum(high, zz * plane + plane - 1)

    def chip_wants(b, o=0):
        chip_low, chip_high = needed(seq_of(z, (y + o) % mid, 0), 2)
        return (b >= chip_low) & (b <= chip_high)

    low, high = bounds(z)
    low_up, _ = bounds(z + 1)
    _, high_down = bounds(z - 1)

    partners = [(p, seq_of(z, y, 1 - c))]
    partners += [(p, seq_of(z, (y + o) % mid, cc)) for o in range(1, mid) for cc in (c, 1 - c)]
    partners += [(p, seq_of((z + o) % slow, y, c)) for o in range(1, slow)]
    partners += [((p + o) % phases, s) for o in range(1, phases)]
    barrier = pltpu.get_barrier_semaphore()
    for target in partners:
        pl.semaphore_signal(barrier, inc=1, device_id=target, device_id_type=MESH)
    loads = [
        pltpu.make_async_copy(source, target, load_sem.at[2 + i])
        for i, (source, target) in enumerate([
            (durations_hbm, durations), (tokens_hbm, tokens), (gain_hbm, gain),
            (unit_gain_hbm, unit_gain)])
    ]
    for load in loads:
        load.start()
    load_w = pltpu.make_async_copy(weight.at[0], w_buf, load_sem.at[0])
    load_w.start()
    load_wu = pltpu.make_async_copy(unit_weight, wu_buf, load_sem.at[1])

    loads[0].wait()
    source = lax.broadcasted_iota(jnp.int32, (rows, 2 * rows), 0)
    lane = lax.broadcasted_iota(jnp.int32, (rows, 2 * rows), 1)
    place = (lane == source + c * rows).astype(BF)
    own = jnp.broadcast_to(durations[...], (8, rows)).astype(F32).astype(BF)
    own = jnp.dot(own, place, preferred_element_type=F32).astype(jnp.int32)
    dur_all[s] = own[0:1, :]

    for b in range(seqsize):
        @pl.when(jnp.logical_not(chip_wants(b)))
        def _():
            held[b * rows:(b + 1) * rows, :] = jnp.zeros((rows, width), BF)

    pl.semaphore_wait(barrier, len(partners))

    def dur_copy(start, size, sem, recv, target):
        return pltpu.make_async_remote_copy(
            src_ref=dur_all.at[pl.ds(start, size)], dst_ref=dur_all.at[pl.ds(start, size)],
            send_sem=sem, recv_sem=recv, device_id=target, device_id_type=MESH)

    def near(i):
        return dur_copy(s, 1, dur_send.at[i], dur_near.at[i], (p, seq_of(
            z, (y + (i + 1) // 2) % mid, (c + i + 1) % 2)))

    for i in range(plane - 1):
        near(i).start()

    def layer_chunks(source_ref, w_ref, gain_row, emit):
        v = source_ref[...].astype(F32)
        scale = lax.rsqrt(jnp.mean(v * v, axis=-1, keepdims=True) + 1e-06)
        normed = (v * gain_row * scale).astype(BF)
        for n in range(chunks):
            part = slice(n * COLS, (n + 1) * COLS)
            x = jnp.dot(normed, w_ref[:, part], preferred_element_type=F32)
            branch = 0.5 * x * (1.0 + jnp.tanh(0.5 * x))
            emit(n, part, (source_ref[:, part].astype(F32) + branch).astype(BF))

    def relay_copy(n):
        part = slice(n * COLS, (n + 1) * COLS)
        return pltpu.make_async_remote_copy(
            src_ref=h_out.at[:, part], dst_ref=h_in.at[:, part],
            send_sem=relay_send.at[n], recv_sem=relay_recv.at[n],
            device_id=((p + 1) % phases, s), device_id_type=MESH)

    def fin_copy(n, o):
        part = slice(n * COLS, (n + 1) * COLS)
        return pltpu.make_async_remote_copy(
            src_ref=h_fin.at[:, part], dst_ref=h_fin.at[:, part],
            send_sem=fin_send.at[n, o - 1], recv_sem=fin_recv.at[n],
            device_id=((p + o) % phases, s), device_id_type=MESH)

    def relay_emit(n, part, value):
        h_out[:, part] = value
        relay_copy(n).start()

    def fin_emit(n, part, value):
        h_fin[:, part] = value
        for o in range(1, phases):
            fin_copy(n, o).start()

    for load in loads[1:]:
        load.wait()
    load_w.wait()
    load_wu.start()

    @pl.when(p == 0)
    def _():
        layer_chunks(tokens, w_buf, gain[...], relay_emit if phases > 1 else fin_emit)

    def far(o):
        return dur_copy(z * plane, plane, dur_send.at[plane - 1 + o], dur_recv.at[o],
                        (p, seq_of((z + o) % slow, y, c)))

    for i in range(plane - 1):
        near(i).wait()
    for o in range(1, slow):
        far(o).start()

    def make_member():
        for o in range(1, slow):
            far(o).wait()
        pairs = seqsize // 2
        for q in range(pairs):
            durs_buf[q:q + 1, :] = (dur_all[2 * q] + dur_all[2 * q + 1]).astype(F32)
        durs = durs_buf[...]
        tri = (lax.broadcasted_iota(jnp.int32, (2 * rows, 2 * rows), 0)
               <= lax.broadcasted_iota(jnp.int32, (2 * rows, 2 * rows), 1)).astype(BF)
        inner = jnp.dot(durs.astype(BF), tri, preferred_element_type=F32)
        frame = (lax.broadcasted_iota(jnp.int32, (FR_DEV, 2 * rows), 0)
                 + (p * seqsize + s) * FR_DEV).astype(F32)
        before = jnp.zeros((1, 1), F32)
        for q in range(pairs):
            ends = inner[q:q + 1, :] + before
            begins = ends - durs[q:q + 1, :]
            inside = jnp.where((frame >= begins) & (frame < ends), 1.0, 0.0).astype(BF)
            at = (q % mid) * 2 * rows
            member[q // mid, :, at:at + 2 * rows] = inside
            before = before + jnp.sum(durs[q:q + 1, :], axis=1, keepdims=True)

    pl.when(jnp.logical_not(last))(make_member)

    if phases > 1:
        @pl.when(p > 0)
        def _():
            for n in range(chunks):
                relay_copy(n).wait_recv()

            @pl.when(jnp.logical_not(last))
            def _():
                layer_chunks(h_in, w_buf, gain[...], relay_emit)

            @pl.when(last)
            def _():
                layer_chunks(h_in, w_buf, gain[...], fin_emit)

        @pl.when(jnp.logical_not(last))
        def _():
            for n in range(chunks):
                fin_copy(n, 1).wait_recv()

    enc_copy = pltpu.make_async_copy(h_fin, enc_out, out_sem.at[0])
    enc_copy.start()

    half = width // HALVES

    def block(b, h):
        return held.at[pl.ds(pl.multiple_of(b * rows, rows), rows), h * half:(h + 1) * half]

    def send(b, h, sem, target):
        return pltpu.make_async_remote_copy(
            src_ref=block(b, h), dst_ref=block(b, h), send_sem=sem, recv_sem=recv_sem.at[b, h],
            device_id=target, device_id_type=MESH)

    def up(zz, h):
        return send(seq_of(zz, y, c), h, up_send.at[zz, h], (p, seq_of((z + 1) % slow, y, c)))

    def down(zz, h):
        return send(seq_of(zz, y, c), h, down_send.at[zz, h],
                    (p, seq_of((z + slow - 1) % slow, y, c)))

    def across(zz, o, h):
        return send(seq_of(zz, y, c), h, mid_send.at[zz, o, h], (p, seq_of(z, (y + o) % mid, c)))

    def sibling(b, h):
        return send(b, h, pair_send.at[b, h], (p, seq_of(z, y, 1 - c)))

    def arrived(b, h):
        sibling(b, h).wait_recv()

    def goes_up(zz):
        return (z + 1 < slow) & (zz <= z) & (seq_of(zz, y, c) >= low_up)

    def goes_down(zz):
        return (z > 0) & (zz >= z) & (seq_of(zz, y, c) <= high_down)

    def wanted(b):
        return (b >= low) & (b <= high)

    def valid(zz):
        return (zz >= 0) & (zz < slow)

    def spread_column(zz, h):
        @pl.when(goes_up(zz))
        def _():
            up(zz, h).start()

        @pl.when(goes_down(zz))
        def _():
            down(zz, h).start()

        b = seq_of(zz, y, c)
        for o in range(1, mid):
            @pl.when(chip_wants(b, o))
            def _():
                across(zz, o, h).start()

        @pl.when(chip_wants(b))
        def _():
            sibling(b, h).start()

    load_wu.wait()

    def unit_emit(n, part, value):
        held[pl.ds(pl.multiple_of(s * rows, rows), rows), part] = value
        if (n + 1) * COLS % half == 0:
            spread_column(z, n * COLS // half)

    layer_chunks(h_fin, wu_buf, unit_gain[...], unit_emit)

    def column(zz, h):
        b = seq_of(zz, y, c)

        @pl.when(valid(zz) & wanted(b))
        def _():
            arrived(b, h)
            spread_column(zz, h)

    def from_across(zz, h):
        for o in range(1, mid):
            b = seq_of(zz, (y + o) % mid, c)

            @pl.when(valid(zz) & chip_wants(b))
            def _():
                arrived(b, h)
                sibling(b, h).start()

    def add_plane(zz, h, first):
        def work():
            for yy in range(mid):
                b = seq_of(zz, yy, 1 - c)

                @pl.when(chip_wants(b))
                def _():
                    arrived(b, h)

            mask = member[zz]
            rows_at = pl.ds(pl.multiple_of(zz * plane * rows, plane * rows), plane * rows)
            for n in range(h * half // COLS, (h + 1) * half // COLS):
                cols = slice(n * COLS, (n + 1) * COLS)
                got = jnp.dot(mask, held[rows_at, cols], preferred_element_type=F32)
                if first:
                    total[:, cols] = got
                else:
                    total[:, cols] += got

        if first:
            work()
        else:
            chip_low, chip_high = needed(seq_of(z, y, 0), 2)
            pl.when(valid(zz) & (zz * plane + plane - 1 >= chip_low)
                    & (zz * plane <= chip_high))(work)

    pl.when(last)(make_member)
    out_copies = []
    steps = [(k, h) for k in range(slow) for h in range(HALVES)]
    for i in range(HALVES, len(steps) + 4):
        if i < len(steps):
            k, h = steps[i]
            column(z - k, h)
            column(z + k, h)
        if i == HALVES:
            for h in range(HALVES - 1):
                from_across(z, h)
        if i - 1 < len(steps):
            k, h = steps[i - 1]
            for zz in (z - k, z + k) if k else (z,):
                from_across(zz, h)
        if 0 <= i - 4 < len(steps):
            k, h = steps[i - 4]
            for zz in (z - k, z + k) if k else (z,):
                add_plane(zz, h, k == 0)
            if k == slow - 1:
                part = slice(h * half, (h + 1) * half)
                o_buf[:, part] = total[:, part].astype(BF)
                copy = pltpu.make_async_copy(o_buf.at[:, part], unit_out.at[:, part],
                                             out_sem.at[1 + h])
                copy.start()
                out_copies.append(copy)

    if phases > 1:
        @pl.when(jnp.logical_not(last))
        def _():
            for n in range(chunks):
                relay_copy(n).wait_send()

        @pl.when(last)
        def _():
            for n in range(chunks):
                for o in range(1, phases):
                    fin_copy(n, o).wait_send()

    for zz in range(slow):
        @pl.when(wanted(seq_of(zz, y, c)))
        def _():
            for h in range(HALVES):
                @pl.when(goes_up(zz))
                def _():
                    up(zz, h).wait_send()

                @pl.when(goes_down(zz))
                def _():
                    down(zz, h).wait_send()

                for o in range(1, mid):
                    @pl.when(chip_wants(seq_of(zz, y, c), o))
                    def _():
                        across(zz, o, h).wait_send()

        for yy in range(mid):
            b = seq_of(zz, yy, c)

            @pl.when(chip_wants(b))
            def _():
                for h in range(HALVES):
                    sibling(b, h).wait_send()

    enc_copy.wait()
    for copy in out_copies:
        copy.wait()


def shards(tokens, phase_weight, phase_gain, unit_weight, unit_gain, durations):
    phases = lax.axis_size("phase")
    seqsize = lax.axis_size("seq")
    slow, mid = factors(seqsize)
    rows, width = tokens.shape
    chunks = width // COLS
    anywhere = pl.BlockSpec(memory_space=pl.ANY)
    hbm = pl.BlockSpec(memory_space=pltpu.HBM)
    dma = pltpu.SemaphoreType.DMA
    return pl.pallas_call(
        functools.partial(kernel, phases, seqsize, slow, mid, rows),
        out_shape=(
            pltpu.VMEM((rows, width), BF),
            pltpu.VMEM((FR_DEV, width), BF),
        ),
        in_specs=[hbm] * 6,
        out_specs=(anywhere, anywhere),
        scratch_shapes=[
            pltpu.VMEM((rows, width), BF),
            pltpu.VMEM((1, width), F32),
            pltpu.VMEM((1, width), F32),
            pltpu.VMEM((1, rows), jnp.int32),
            pltpu.VMEM((width, width), BF),
            pltpu.VMEM((width, width), BF),
            pltpu.VMEM((rows, width), BF),
            pltpu.VMEM((rows, width), BF),
            pltpu.VMEM((rows, width), BF),
            pltpu.VMEM((rows * seqsize, width), BF),
            pltpu.VMEM((slow, FR_DEV, 2 * mid * rows), BF),
            pltpu.VMEM((FR_DEV, width), F32),
            pltpu.VMEM((FR_DEV, width), BF),
            pltpu.VMEM((seqsize, 1, 2 * rows), jnp.int32),
            pltpu.VMEM((seqsize // 2, 2 * rows), F32),
            dma((6,)),
            dma((5,)),
            dma((chunks,)),
            dma((chunks,)),
            dma((chunks, max(phases - 1, 1))),
            dma((chunks,)),
            dma((2 * mid + slow,)),
            dma((2 * mid,)),
            dma((slow,)),
            dma((slow, HALVES)),
            dma((slow, HALVES)),
            dma((slow, mid, HALVES)),
            dma((seqsize, HALVES)),
            dma((seqsize, HALVES)),
        ],
        compiler_params=pltpu.CompilerParams(
            collective_id=0, has_side_effects=True, vmem_limit_bytes=40 * 1024 * 1024
        ),
        cost_estimate=pl.CostEstimate(
            flops=10 ** 9, bytes_accessed=8 * 10 ** 6, transcendentals=2 * 10 ** 5
        ),
    )(*[pltpu.with_memory_space_constraint(a, pltpu.HBM) for a in (tokens, phase_weight, phase_gain, unit_weight, unit_gain.reshape(1, width),
      durations.reshape(1, rows))])


def solution(mesh):
    return jax.shard_map(
        shards,
        mesh=mesh,
        in_specs=(P("seq", None), P("phase", None, None), P("phase", None), P(), P(), P("seq")),
        out_specs=(P("seq", None), P(("phase", "seq"), None)),
        check_vma=False,
    )
```

```python
import functools

import jax
import jax.numpy as jnp
from jax import lax
from jax.experimental import pallas as pl
from jax.experimental.pallas import tpu as pltpu
from jax.sharding import PartitionSpec as P

FR_DEV = 256
COLS = 256
HALVES = 2
MESH = pl.DeviceIdType.MESH
BF = jnp.bfloat16
F32 = jnp.float32


def factors(seqsize):
    chips = seqsize // 2
    mid = 2 ** ((chips.bit_length() - 1) // 2)
    return chips // mid, mid


def kernel(
    phases, seqsize, slow, mid, rows,
    tokens_hbm, weight, gain_hbm, unit_weight, unit_gain_hbm, durations_hbm,
    enc_out, unit_out,
    tokens, gain, unit_gain, durations, w_buf, wu_buf, h_in, h_out, h_fin, held, member, total, o_buf, dur_all, durs_buf,
    load_sem, out_sem, relay_send, relay_recv, fin_send, fin_recv,
    dur_send, dur_near, dur_recv, up_send, down_send, mid_send, pair_send, recv_sem,
):
    width = tokens.shape[1]
    chunks = width // COLS
    plane = 2 * mid
    p = lax.axis_index("phase")
    s = lax.axis_index("seq")
    z = s // plane
    y = (s // 2) % mid
    c = s % 2
    last = p == phases - 1
    everyone = phases * seqsize
    frames = everyone * FR_DEV
    toks = rows * seqsize
    dmin = frames // (2 * toks)
    dmax = 8 * dmin

    def seq_of(zz, yy, cc):
        return zz * plane + yy * 2 + cc

    def needed(first, count):
        f0 = (p * seqsize + first) * FR_DEV
        f1 = f0 + count * FR_DEV - 1
        low = jnp.maximum(f0 // dmax, toks - (frames - f0) // dmin)
        high = jnp.minimum(f1 // dmin, toks - ((frames - f1 - 1) // dmax + 1))
        return low // rows, high // rows

    def bounds(zz):
        low, high = needed(zz * plane, plane)
        return jnp.minimum(low, zz * plane), jnp.maximum(high, zz * plane + plane - 1)

    def chip_wants(b, o=0):
        chip_low, chip_high = needed(seq_of(z, (y + o) % mid, 0), 2)
        return (b >= chip_low) & (b <= chip_high)

    low, high = bounds(z)
    low_up, _ = bounds(z + 1)
    _, high_down = bounds(z - 1)

    partners = [(p, seq_of(z, y, 1 - c))]
    partners += [(p, seq_of(z, (y + o) % mid, cc)) for o in range(1, mid) for cc in (c, 1 - c)]
    partners += [(p, seq_of((z + o) % slow, y, c)) for o in range(1, slow)]
    partners += [((p + o) % phases, s) for o in range(1, phases)]
    barrier = pltpu.get_barrier_semaphore()
    for target in partners:
        pl.semaphore_signal(barrier, inc=1, device_id=target, device_id_type=MESH)
    loads = [
        pltpu.make_async_copy(source, target, load_sem.at[2 + i])
        for i, (source, target) in enumerate([
            (durations_hbm, durations), (tokens_hbm, tokens), (gain_hbm, gain),
            (unit_gain_hbm, unit_gain)])
    ]
    for load in loads:
        load.start()
    load_w = pltpu.make_async_copy(weight.at[0], w_buf, load_sem.at[0])
    load_w.start()
    load_wu = pltpu.make_async_copy(unit_weight, wu_buf, load_sem.at[1])

    loads[0].wait()
    source = lax.broadcasted_iota(jnp.int32, (rows, 2 * rows), 0)
    lane = lax.broadcasted_iota(jnp.int32, (rows, 2 * rows), 1)
    place = (lane == source + c * rows).astype(BF)
    own = jnp.broadcast_to(durations[...], (8, rows)).astype(F32).astype(BF)
    own = jnp.dot(own, place, preferred_element_type=F32).astype(jnp.int32)
    dur_all[s] = own[0:1, :]

    for b in range(seqsize):
        @pl.when(jnp.logical_not(chip_wants(b)))
        def _():
            held[b * rows:(b + 1) * rows, :] = jnp.zeros((rows, width), BF)

    pl.semaphore_wait(barrier, len(partners))

    def dur_copy(start, size, sem, recv, target):
        return pltpu.make_async_remote_copy(
            src_ref=dur_all.at[pl.ds(start, size)], dst_ref=dur_all.at[pl.ds(start, size)],
            send_sem=sem, recv_sem=recv, device_id=target, device_id_type=MESH)

    def near(i):
        return dur_copy(s, 1, dur_send.at[i], dur_near.at[i], (p, seq_of(
            z, (y + (i + 1) // 2) % mid, (c + i + 1) % 2)))

    for i in range(plane - 1):
        near(i).start()

    def layer_chunks(source_ref, w_ref, gain_row, emit):
        v = source_ref[...].astype(F32)
        scale = lax.rsqrt(jnp.mean(v * v, axis=-1, keepdims=True) + 1e-06)
        normed = (v * gain_row * scale).astype(BF)
        for n in range(chunks):
            part = slice(n * COLS, (n + 1) * COLS)
            x = jnp.dot(normed, w_ref[:, part], preferred_element_type=F32)
            branch = 0.5 * x * (1.0 + jnp.tanh(0.5 * x))
            emit(n, part, (source_ref[:, part].astype(F32) + branch).astype(BF))

    def relay_copy(n):
        part = slice(n * COLS, (n + 1) * COLS)
        return pltpu.make_async_remote_copy(
            src_ref=h_out.at[:, part], dst_ref=h_in.at[:, part],
            send_sem=relay_send.at[n], recv_sem=relay_recv.at[n],
            device_id=((p + 1) % phases, s), device_id_type=MESH)

    def fin_copy(n, o):
        part = slice(n * COLS, (n + 1) * COLS)
        return pltpu.make_async_remote_copy(
            src_ref=h_fin.at[:, part], dst_ref=h_fin.at[:, part],
            send_sem=fin_send.at[n, o - 1], recv_sem=fin_recv.at[n],
            device_id=((p + o) % phases, s), device_id_type=MESH)

    def relay_emit(n, part, value):
        h_out[:, part] = value
        relay_copy(n).start()

    def fin_emit(n, part, value):
        h_fin[:, part] = value
        for o in range(1, phases):
            fin_copy(n, o).start()

    for load in loads[1:]:
        load.wait()
    load_w.wait()
    load_wu.start()

    @pl.when(p == 0)
    def _():
        layer_chunks(tokens, w_buf, gain[...], relay_emit if phases > 1 else fin_emit)

    def far(o):
        return dur_copy(z * plane, plane, dur_send.at[plane - 1 + o], dur_recv.at[o],
                        (p, seq_of((z + o) % slow, y, c)))

    for i in range(plane - 1):
        near(i).wait()
    for o in range(1, slow):
        far(o).start()

    def make_member():
        for o in range(1, slow):
            far(o).wait()
        pairs = seqsize // 2
        for q in range(pairs):
            durs_buf[q:q + 1, :] = (dur_all[2 * q] + dur_all[2 * q + 1]).astype(F32)
        durs = durs_buf[...]
        tri = (lax.broadcasted_iota(jnp.int32, (2 * rows, 2 * rows), 0)
               <= lax.broadcasted_iota(jnp.int32, (2 * rows, 2 * rows), 1)).astype(BF)
        inner = jnp.dot(durs.astype(BF), tri, preferred_element_type=F32)
        frame = (lax.broadcasted_iota(jnp.int32, (FR_DEV, 2 * rows), 0)
                 + (p * seqsize + s) * FR_DEV).astype(F32)
        before = jnp.zeros((1, 1), F32)
        for q in range(pairs):
            ends = inner[q:q + 1, :] + before
            begins = ends - durs[q:q + 1, :]
            inside = jnp.where((frame >= begins) & (frame < ends), 1.0, 0.0).astype(BF)
            at = (q % mid) * 2 * rows
            member[q // mid, :, at:at + 2 * rows] = inside
            before = before + jnp.sum(durs[q:q + 1, :], axis=1, keepdims=True)

    pl.when(jnp.logical_not(last))(make_member)

    if phases > 1:
        @pl.when(p > 0)
        def _():
            for n in range(chunks):
                relay_copy(n).wait_recv()

            @pl.when(jnp.logical_not(last))
            def _():
                layer_chunks(h_in, w_buf, gain[...], relay_emit)

            @pl.when(last)
            def _():
                layer_chunks(h_in, w_buf, gain[...], fin_emit)

        @pl.when(jnp.logical_not(last))
        def _():
            for n in range(chunks):
                fin_copy(n, 1).wait_recv()

    enc_copy = pltpu.make_async_copy(h_fin, enc_out, out_sem.at[0])
    enc_copy.start()

    half = width // HALVES

    def block(b, h):
        return held.at[pl.ds(pl.multiple_of(b * rows, rows), rows), h * half:(h + 1) * half]

    def send(b, h, sem, target):
        return pltpu.make_async_remote_copy(
            src_ref=block(b, h), dst_ref=block(b, h), send_sem=sem, recv_sem=recv_sem.at[b, h],
            device_id=target, device_id_type=MESH)

    def up(zz, h):
        return send(seq_of(zz, y, c), h, up_send.at[zz, h], (p, seq_of((z + 1) % slow, y, c)))

    def down(zz, h):
        return send(seq_of(zz, y, c), h, down_send.at[zz, h],
                    (p, seq_of((z + slow - 1) % slow, y, c)))

    def across(zz, o, h):
        return send(seq_of(zz, y, c), h, mid_send.at[zz, o, h], (p, seq_of(z, (y + o) % mid, c)))

    def sibling(b, h):
        return send(b, h, pair_send.at[b, h], (p, seq_of(z, y, 1 - c)))

    def arrived(b, h):
        sibling(b, h).wait_recv()

    def goes_up(zz):
        return (z + 1 < slow) & (zz <= z) & (seq_of(zz, y, c) >= low_up)

    def goes_down(zz):
        return (z > 0) & (zz >= z) & (seq_of(zz, y, c) <= high_down)

    def wanted(b):
        return (b >= low) & (b <= high)

    def valid(zz):
        return (zz >= 0) & (zz < slow)

    def spread_column(zz, h):
        @pl.when(goes_up(zz))
        def _():
            up(zz, h).start()

        @pl.when(goes_down(zz))
        def _():
            down(zz, h).start()

        b = seq_of(zz, y, c)
        for o in range(1, mid):
            @pl.when(chip_wants(b, o))
            def _():
                across(zz, o, h).start()

        @pl.when(chip_wants(b))
        def _():
            sibling(b, h).start()

    load_wu.wait()

    def unit_emit(n, part, value):
        held[pl.ds(pl.multiple_of(s * rows, rows), rows), part] = value
        if (n + 1) * COLS % half == 0:
            spread_column(z, n * COLS // half)

    layer_chunks(h_fin, wu_buf, unit_gain[...], unit_emit)

    def column(zz, h):
        b = seq_of(zz, y, c)

        @pl.when(valid(zz) & wanted(b))
        def _():
            arrived(b, h)
            spread_column(zz, h)

    def from_across(zz, h):
        for o in range(1, mid):
            b = seq_of(zz, (y + o) % mid, c)

            @pl.when(valid(zz) & chip_wants(b))
            def _():
                arrived(b, h)
                sibling(b, h).start()

    def add_plane(zz, h, first):
        def work():
            for yy in range(mid):
                b = seq_of(zz, yy, 1 - c)

                @pl.when(chip_wants(b))
                def _():
                    arrived(b, h)

            mask = member[zz]
            rows_at = pl.ds(pl.multiple_of(zz * plane * rows, plane * rows), plane * rows)
            for n in range(h * half // COLS, (h + 1) * half // COLS):
                cols = slice(n * COLS, (n + 1) * COLS)
                got = jnp.dot(mask, held[rows_at, cols], preferred_element_type=F32)
                if first:
                    total[:, cols] = got
                else:
                    total[:, cols] += got

        if first:
            work()
        else:
            chip_low, chip_high = needed(seq_of(z, y, 0), 2)
            pl.when(valid(zz) & (zz * plane + plane - 1 >= chip_low)
                    & (zz * plane <= chip_high))(work)

    pl.when(last)(make_member)
    out_copies = []
    steps = [(k, h) for k in range(slow) for h in range(HALVES)]
    for i in range(HALVES, len(steps) + 5):
        if i < len(steps):
            k, h = steps[i]
            column(z - k, h)
            column(z + k, h)
        if 0 <= i - 2 < len(steps):
            k, h = steps[i - 2]
            for zz in (z - k, z + k) if k else (z,):
                from_across(zz, h)
        if 0 <= i - 5 < len(steps):
            k, h = steps[i - 5]
            for zz in (z - k, z + k) if k else (z,):
                add_plane(zz, h, k == 0)
            if k == slow - 1:
                part = slice(h * half, (h + 1) * half)
                o_buf[:, part] = total[:, part].astype(BF)
                copy = pltpu.make_async_copy(o_buf.at[:, part], unit_out.at[:, part],
                                             out_sem.at[1 + h])
                copy.start()
                out_copies.append(copy)

    if phases > 1:
        @pl.when(jnp.logical_not(last))
        def _():
            for n in range(chunks):
                relay_copy(n).wait_send()

        @pl.when(last)
        def _():
            for n in range(chunks):
                for o in range(1, phases):
                    fin_copy(n, o).wait_send()

    for zz in range(slow):
        @pl.when(wanted(seq_of(zz, y, c)))
        def _():
            for h in range(HALVES):
                @pl.when(goes_up(zz))
                def _():
                    up(zz, h).wait_send()

                @pl.when(goes_down(zz))
                def _():
                    down(zz, h).wait_send()

                for o in range(1, mid):
                    @pl.when(chip_wants(seq_of(zz, y, c), o))
                    def _():
                        across(zz, o, h).wait_send()

        for yy in range(mid):
            b = seq_of(zz, yy, c)

            @pl.when(chip_wants(b))
            def _():
                for h in range(HALVES):
                    sibling(b, h).wait_send()

    enc_copy.wait()
    for copy in out_copies:
        copy.wait()


def shards(tokens, phase_weight, phase_gain, unit_weight, unit_gain, durations):
    phases = lax.axis_size("phase")
    seqsize = lax.axis_size("seq")
    slow, mid = factors(seqsize)
    rows, width = tokens.shape
    chunks = width // COLS
    anywhere = pl.BlockSpec(memory_space=pl.ANY)
    hbm = pl.BlockSpec(memory_space=pltpu.HBM)
    dma = pltpu.SemaphoreType.DMA
    return pl.pallas_call(
        functools.partial(kernel, phases, seqsize, slow, mid, rows),
        out_shape=(
            pltpu.VMEM((rows, width), BF),
            pltpu.VMEM((FR_DEV, width), BF),
        ),
        in_specs=[hbm] * 6,
        out_specs=(anywhere, anywhere),
        scratch_shapes=[
            pltpu.VMEM((rows, width), BF),
            pltpu.VMEM((1, width), F32),
            pltpu.VMEM((1, width), F32),
            pltpu.VMEM((1, rows), jnp.int32),
            pltpu.VMEM((width, width), BF),
            pltpu.VMEM((width, width), BF),
            pltpu.VMEM((rows, width), BF),
            pltpu.VMEM((rows, width), BF),
            pltpu.VMEM((rows, width), BF),
            pltpu.VMEM((rows * seqsize, width), BF),
            pltpu.VMEM((slow, FR_DEV, 2 * mid * rows), BF),
            pltpu.VMEM((FR_DEV, width), F32),
            pltpu.VMEM((FR_DEV, width), BF),
            pltpu.VMEM((seqsize, 1, 2 * rows), jnp.int32),
            pltpu.VMEM((seqsize // 2, 2 * rows), F32),
            dma((6,)),
            dma((5,)),
            dma((chunks,)),
            dma((chunks,)),
            dma((chunks, max(phases - 1, 1))),
            dma((chunks,)),
            dma((2 * mid + slow,)),
            dma((2 * mid,)),
            dma((slow,)),
            dma((slow, HALVES)),
            dma((slow, HALVES)),
            dma((slow, mid, HALVES)),
            dma((seqsize, HALVES)),
            dma((seqsize, HALVES)),
        ],
        compiler_params=pltpu.CompilerParams(
            collective_id=0, has_side_effects=True, vmem_limit_bytes=40 * 1024 * 1024
        ),
        cost_estimate=pl.CostEstimate(
            flops=10 ** 9, bytes_accessed=8 * 10 ** 6, transcendentals=2 * 10 ** 5
        ),
    )(*[pltpu.with_memory_space_constraint(a, pltpu.HBM) for a in (tokens, phase_weight, phase_gain, unit_weight, unit_gain.reshape(1, width),
      durations.reshape(1, rows))])


def solution(mesh):
    return jax.shard_map(
        shards,
        mesh=mesh,
        in_specs=(P("seq", None), P("phase", None, None), P("phase", None), P(), P(), P("seq")),
        out_specs=(P("seq", None), P(("phase", "seq"), None)),
        check_vma=False,
    )
```
